1024 devices in a mesh: col: 16 (over x, core), tab: 32 (over z, y_hi), dp: 2 (over y_lo).
Axes of the slice: x: 8, y: 8 (y_hi: 4, y_lo: 2; y = y_hi * 2 + y_lo), z: 8, core: 2. Of those that a mesh axis runs over, the one named last changes fastest.
Arguments:
- wide_rows: bfloat16 [2, 64, 2048, 1024], P(None, ('tab', 'dp'), None, 'col'), may hold values from -6 to 6
- wide_lengths: int32 [2, 64, 512], P(None, ('tab', 'dp')), may hold values from 1 to 12, 2048 in all within a row
- narrow_rows: bfloat16 [32, 32, 4096, 128], P('tab', ('col', 'dp')), may hold values from -6 to 6
- narrow_lengths: int32 [32, 32, 1024], P('tab', ('col', 'dp')), may hold values from 1 to 12, 4096 in all within a row
- narrow_widths: int32 [32], P('tab'), may hold values from 32 to 128
- wide_proj: bfloat16 [2, 1024, 512], P(None, 'col'), may hold values from -0.09375 to 0.09375
- narrow_proj: bfloat16 [32, 128, 512], P('tab'), may hold values from -0.25 to 0.25
- cotangent: bfloat16 [32768, 512], P(('col', 'tab', 'dp')), may hold values from -24 to 24
Outputs:
- cross_input: bfloat16 [32768, 512], P(('col', 'tab', 'dp'))
- wide_row_grads: bfloat16 [2, 64, 2048, 1024], P(None, ('tab', 'dp'), None, 'col')
- narrow_row_grads: bfloat16 [32, 32, 4096, 128], P('tab', ('col', 'dp'))
- wide_proj_grads: float32 [2, 1024, 512], P(None, 'col', ('tab', 'dp'))
- narrow_proj_grads: float32 [32, 128, 512], P('tab', None, ('col', 'dp'))
The draws below stay inside these ranges and needn't reach their ends.
Inputs may be any that keep to these rules, and one draw needn't show every extreme that they name: `wide_lengths`: in each table and block the lengths sum to the block's rows (2048 for wide tables) and some bag has exactly 12 rows. `narrow_lengths`: in each table and block the lengths sum to 4096 and some bag has exactly 12 rows.
All inputs are finite; a program needn't handle non-finite values.
Results may differ from the reference program's by a relative error of at most 0.0049.
Values may be sent and summed in bfloat16 or wider, within the bound.
A program may use at most 32 MiB of HBM per device.

```python
import math
import jax
import jax.numpy as jnp
import numpy as np
from jax import lax

SAMPLES_DEV = 32
WIDE_TABLES = 2
WIDE_DIM = 1024
NARROW_SLOT = 128
EMBED_OUT = 512
BAG_MEAN = 4
BAG_MOST = 12
WIDE_BLOCK = 512
NARROW_BLOCK = 1024
WIDE_ROWS = 2048
NARROW_ROWS = 4096
WIDE_BLOCKS = 64
NARROW_BLOCKS = 32
NARROW_TABLES = 32
SAMPLES = 32768
N_COL = 16
N_TAB = 32
N_DP = 2


def place_ends(entries, key, low, high):
    extent = entries.shape
    index_at = [jax.random.randint(jax.random.fold_in(key, axis), (), 0, extent[axis]) for axis in range(len(extent))]
    entries = entries.at[tuple(index_at)].set(low)
    longest = extent.index(max(extent))
    index_at[longest] = (index_at[longest] + 1) % extent[longest]
    return entries.at[tuple(index_at)].set(high)


def strengthened(drawn, key, source, target, shards_of, factor):
    owner, partner = [(jnp.arange(drawn.shape[position]) // (drawn.shape[position] // shards_of)).reshape([-1 if axis == position else 1 for axis in range(drawn.ndim)]) for position in (source, target)]
    chosen = jax.random.permutation(key, shards_of)[partner]
    strong = (owner == chosen) | (owner == (partner + shards_of // 2) % shards_of)
    return jnp.where(strong, factor * drawn, drawn)


def steps_of(stream_key, shape, split, least, largest):
    gain, own = 1.0, jax.random.fold_in(stream_key, 6)
    for axis_at, shards_of in split:
        heights = jnp.exp(jax.random.uniform(jax.random.fold_in(own, axis_at), (shards_of,), jnp.float32, least / len(split), largest / len(split)))
        gain = gain * jnp.repeat(heights, shape[axis_at] // shards_of).reshape([-1 if axis == axis_at else 1 for axis in range(len(shape))])
    return gain


def split_up(amount, total, bound, lean):
    portions = [(1 << 20) // math.isqrt(standing ** lean) + 1 for standing in range(2, amount + 1)]
    spare, holding = total - bound - (amount - 1), [1] * (amount - 1)
    while spare > 0:
        candidates = [i for i in range(amount - 1) if holding[i] < bound]
        pool, left = sum([portions[i] for i in candidates]), spare
        for i in candidates:
            more = min(bound - holding[i], max(1, left * portions[i] // pool), spare)
            holding[i] = holding[i] + more
            spare = spare - more
    return np.array([bound] + holding)


def uneven(own_key, count, total, most, slope):
    if count == 2:
        one = jax.random.randint(own_key, (), max(1, total - most), min(most, total - 1) + 1)
        return jnp.stack([one, total - one])
    tallies = jnp.asarray(split_up(count, total, most, slope), jnp.int32)
    pairs = (count - 1) // 2
    donor, receiver = tallies[1:1 + 2 * pairs:2], tallies[2:2 + 2 * pairs:2]
    slack = jnp.minimum(donor - 1, most - receiver)
    moved = jax.random.randint(jax.random.fold_in(own_key, 1), (pairs,), 0, 1 << 20) % (slack + 1)
    tallies = tallies.at[1:1 + 2 * pairs:2].set(donor - moved).at[2:2 + 2 * pairs:2].set(receiver + moved)
    return tallies[jax.random.permutation(jax.random.fold_in(own_key, 2), count)]


def gaussian(key, dims, spread, reach, cuts=(), kind=jnp.bfloat16):
    drawn = jax.random.normal(key, dims, jnp.float32) * spread
    if len(cuts) > 0:
        drawn = steps_of(key, dims, cuts, -0.22, 0.18) * drawn
    return jnp.clip(drawn, min=-reach, max=reach).astype(kind)


def bell_draw_with(rng, extent, spread, most, cuts, heavy, kind=jnp.bfloat16):
    drawn = spread * jax.random.normal(rng, extent, jnp.float32)
    if cuts:
        drawn = drawn * steps_of(rng, extent, cuts, -0.22, 0.18)
    return jnp.clip(strengthened(drawn, jax.random.fold_in(rng, 3), *heavy), -most, most).astype(kind)


def setup_inputs(seed: int = 0) -> dict:
    keys = jax.random.split(jax.random.key(seed), 9)
    return {
        "wide_rows": gaussian(keys[0], (WIDE_TABLES, WIDE_BLOCKS, WIDE_ROWS, WIDE_DIM), 1.0, 6.0, ((1, 64), (3, 16))),
        "wide_lengths": jax.vmap(lambda own: uneven(own, WIDE_BLOCK, WIDE_ROWS, BAG_MOST, 1))(jax.random.split(keys[1], WIDE_TABLES * WIDE_BLOCKS)).reshape((WIDE_TABLES, WIDE_BLOCKS, WIDE_BLOCK)).astype(jnp.int32),
        "narrow_rows": gaussian(keys[2], (NARROW_TABLES, NARROW_BLOCKS, NARROW_ROWS, NARROW_SLOT), 1.0, 6.0, ((0, 32), (1, 32))),
        "narrow_lengths": jax.vmap(lambda own: uneven(own, NARROW_BLOCK, NARROW_ROWS, BAG_MOST, 1))(jax.random.split(keys[3], NARROW_TABLES * NARROW_BLOCKS)).reshape((NARROW_TABLES, NARROW_BLOCKS, NARROW_BLOCK)).astype(jnp.int32),
        "narrow_widths": place_ends(jax.random.randint(keys[4], (NARROW_TABLES,), NARROW_SLOT // 4, NARROW_SLOT + 1), jax.random.fold_in(keys[4], 1), NARROW_SLOT // 4, NARROW_SLOT).astype(jnp.int32),
        "wide_proj": gaussian(keys[5], (WIDE_TABLES, WIDE_DIM, EMBED_OUT), (BAG_MEAN * WIDE_DIM) ** -0.5, 0.09375, ((1, 16),)),
        "narrow_proj": gaussian(keys[6], (NARROW_TABLES, NARROW_SLOT, EMBED_OUT), (BAG_MEAN * NARROW_SLOT) ** -0.5, 0.25, ((0, 32),)),
        "cotangent": bell_draw_with(keys[7], (SAMPLES, EMBED_OUT), 1.0, 24.0, ((0, 1024),), (0, 1, 512, 6.0)),
    }


def bag_ids(lengths, count):
    ends = jnp.cumsum(lengths).astype(jnp.int32)
    return jnp.searchsorted(ends, jnp.arange(count, dtype=jnp.int32), side="right").astype(jnp.int32)


def pool_block(rows, lengths):
    ids = bag_ids(lengths, rows.shape[0])
    summed = jax.ops.segment_sum(rows.astype(jnp.float32), ids, num_segments=lengths.shape[0])
    return summed, ids


def wide_order(values):
    width = values.shape[-1]
    shaped = values.reshape(N_TAB, N_DP, N_COL, SAMPLES_DEV, width)
    return shaped.transpose(2, 0, 1, 3, 4).reshape(SAMPLES, width)


def wide_blocks(values):
    width = values.shape[-1]
    shaped = values.reshape(N_COL, N_TAB, N_DP, SAMPLES_DEV, width)
    return shaped.transpose(1, 2, 0, 3, 4).reshape(WIDE_BLOCKS, WIDE_BLOCK, width)


def narrow_order(values):
    width = values.shape[-1]
    shaped = values.reshape(N_COL, N_DP, N_TAB, SAMPLES_DEV, width)
    return shaped.transpose(0, 2, 1, 3, 4).reshape(SAMPLES, width)


def narrow_blocks(values):
    width = values.shape[-1]
    shaped = values.reshape(N_COL, N_TAB, N_DP, SAMPLES_DEV, width)
    return shaped.transpose(0, 2, 1, 3, 4).reshape(NARROW_BLOCKS, NARROW_BLOCK, width)


def pick_rows(back, ids):
    return back[ids]


def reference(wide_rows, wide_lengths, narrow_rows, narrow_lengths, narrow_widths, wide_proj, narrow_proj, cotangent):
    factor = (WIDE_TABLES + NARROW_TABLES) ** -0.5

    def wide_table(term, inputs):
        rows, lengths, proj = inputs
        summed, ids = jax.vmap(pool_block)(rows, lengths)
        pooled = wide_order(summed.astype(jnp.bfloat16))
        term = term + factor * jnp.dot(pooled, proj, preferred_element_type=jnp.float32)
        grads = factor * jnp.dot(pooled.T, cotangent, preferred_element_type=jnp.float32)
        back = (factor * jnp.dot(cotangent, proj.T, preferred_element_type=jnp.float32)).astype(jnp.bfloat16)
        row_grads = jax.vmap(pick_rows)(wide_blocks(back), ids)
        return term, (row_grads, grads)

    def narrow_table(term, inputs):
        rows, lengths, width, proj = inputs
        keep = jnp.arange(NARROW_SLOT, dtype=jnp.int32) < width
        summed, ids = jax.vmap(pool_block)(rows, lengths)
        summed = jnp.where(keep[None, None, :], summed, 0.0)
        pooled = narrow_order(summed.astype(jnp.bfloat16))
        term = term + factor * jnp.dot(pooled, proj, preferred_element_type=jnp.float32)
        grads = factor * jnp.dot(pooled.T, cotangent, preferred_element_type=jnp.float32)
        back = factor * jnp.dot(cotangent, proj.T, preferred_element_type=jnp.float32)
        back = jnp.where(keep[None, :], back, 0.0).astype(jnp.bfloat16)
        row_grads = jax.vmap(pick_rows)(narrow_blocks(back), ids)
        return term, (row_grads, grads)

    start = jnp.zeros((SAMPLES, EMBED_OUT), jnp.float32)
    term, (wide_row_grads, wide_proj_grads) = lax.scan(wide_table, start, (wide_rows, wide_lengths, wide_proj))
    term, (narrow_row_grads, narrow_proj_grads) = lax.scan(narrow_table, term, (narrow_rows, narrow_lengths, narrow_widths, narrow_proj))
    return term.astype(jnp.bfloat16), wide_row_grads, narrow_row_grads, wide_proj_grads, narrow_proj_grads
```

```python
import functools

import jax
import jax.numpy as jnp
from jax import lax
from jax.experimental import pallas as pl
from jax.experimental.pallas import tpu as pltpu
from jax.sharding import PartitionSpec as P

MESH = pl.DeviceIdType.MESH
BF = jnp.bfloat16
F32 = jnp.float32

NX, NC, NZ, NY, ND = 8, 2, 8, 4, 2
NYF = NY * ND
PER = 32
CH = NY * PER
LONG, SHORT = 4, 3

NT = (((1,), (1,)), ((), ()))
TN = (((0,), (0,)), ((), ()))
NN = (((1,), (0,)), ((), ()))

A_Y = 0
A_Z = A_Y + NY
R_Z = A_Z + 2 * LONG * NY
X_A = R_Z + 2 * LONG
X_S = X_A + NX
W_S = X_S + 1
W_X = W_S + 1
F_Y = W_X + NX
G_Z = F_Y + NY
G_Y = G_Z + NZ
N_X = G_Y + NYF
N_Q = N_X + NX
N_SEM = N_Q + NC * ND


def dot(a, b, dims):
    return lax.dot_general(a, b, dims, preferred_element_type=F32)


def kernel(
    factor,
    wr_h, wl_h, nr_h, nl_h, nw, wp_h, np_h, cot_h,
    o_x, o_wr, o_nr, o_wg, o_ng,
    wr, wl, nr, nl, wp, npj, cot,
    sb, eb, sr, er, wsb, web,
    pooled, mask, wpooled, wterm, ag, cw,
    rs_out, rs_in, wsib, wx_out, wx_in, fz, fy_out, fy_in,
    wg_out, wg_in, wg2_out, wg2_in, ng_acc, ng_out, ng_in, nq_out, nq_in,
    nrg, wrg, xo, wgo, ngo,
    snd, rcv, isem, osem,
):
    col, tab, dp = lax.axis_index("col"), lax.axis_index("tab"), lax.axis_index("dp")
    x, core = col // NC, lax.rem(col, NC)
    z, y = tab // NY, lax.rem(tab, NY)
    yf = y * ND + dp
    sgn = 1 - 2 * core

    def zz(k):
        return lax.rem(z + sgn * k + 4 * NZ, NZ)

    bar = pltpu.get_barrier_semaphore()

    def hello(**dev):
        pl.semaphore_signal(bar, inc=1, device_id=dev, device_id_type=MESH)

    for k in range(1, NYF):
        p = lax.rem(yf + k, NYF)
        hello(tab=z * NY + p // ND, dp=lax.rem(p, ND))
    for k in range(1, NZ):
        hello(tab=lax.rem(z + k, NZ) * NY + y)
    for k in range(1, NX):
        hello(col=lax.rem(x + k, NX) * NC + core)
    hello(col=x * NC + 1 - core)
    hello(col=x * NC + 1 - core, dp=1 - dp)

    loads = [
        pltpu.make_async_copy(s, d, isem.at[i])
        for i, (s, d) in enumerate(
            [(cot_h, cot), (nl_h, nl), (nr_h, nr), (np_h, npj), (wl_h, wl), (wr_h, wr), (wp_h, wp)]
        )
    ]
    for c in loads:
        c.start()
    l_cot, l_nl, l_nr, l_np, l_wl, l_wr, l_wp = loads

    sent = []

    def copy(src, dst, i, **dev):
        return pltpu.make_async_remote_copy(
            src_ref=src, dst_ref=dst, send_sem=snd.at[i], recv_sem=rcv.at[i],
            device_id=dev, device_id_type=MESH,
        )

    def send(*args, **dev):
        c = copy(*args, **dev)
        c.start()
        sent.append(c)
        return c

    l_cot.wait()
    pl.semaphore_wait(bar, (NYF - 1) + (NZ - 1) + (NX - 1) + 2)

    ay = [None]
    for k in range(1, NY):
        p = lax.rem(y + k, NY)
        ay.append(send(cot, ag.at[z, y], A_Y + k, tab=z * NY + p))
    ag[z, y] = cot[...]
    cw[x, core] = cot[...]

    az = {}

    def forward(step, k):
        q = lax.rem(y - k + NY, NY)
        if step < LONG:
            b = zz(-step)
            az[True, step, k] = send(
                ag.at[b, q], ag.at[b, q], A_Z + step * NY + k, tab=zz(1) * NY + y
            )
        if step < SHORT:
            b = zz(step)
            az[False, step, k] = send(
                ag.at[b, q], ag.at[b, q], A_Z + (LONG + step) * NY + k, tab=zz(-1) * NY + y
            )

    def ring(step):
        for k in range(NY):
            if step > 0:
                az[True, step - 1, k].wait_recv()
                if step - 1 < SHORT:
                    az[False, step - 1, k].wait_recv()
            if step < LONG:
                forward(step, k)

    forward(0, 0)
    xa = [None]
    for k in range(1, NX):
        p = lax.rem(x + k, NX)
        xa.append(send(cot, cw.at[x, core], X_A + k, col=p * NC + core))

    l_nl.wait()
    n_narrow = nl.shape[-1]
    lens = jnp.broadcast_to(nl[0].astype(F32), (CH, n_narrow)).astype(BF)
    for c in range(n_narrow // CH):
        row = lax.broadcasted_iota(jnp.int32, (CH, n_narrow), 0) + c * CH
        place = lax.broadcasted_iota(jnp.int32, (CH, n_narrow), 1)
        upto = jnp.where(place <= row, 1.0, 0.0).astype(BF)
        below = jnp.where(place < row, 1.0, 0.0).astype(BF)
        eb[c] = dot(upto, lens, NT).astype(jnp.int32)
        sb[c] = dot(below, lens, NT).astype(jnp.int32)
        er[c] = dot(lens[:16], upto, NT).astype(jnp.int32)
        sr[c] = dot(lens[:16], below, NT).astype(jnp.int32)

    for k in range(1, NY):
        ay[k].wait_recv()
        forward(0, k)

    l_np.wait()
    l_nr.wait()
    n_rows = nr.shape[2]
    slot = nr.shape[3]
    keep = lax.broadcasted_iota(jnp.int32, (2 * CH, slot), 1) < nw[0]
    lane = lax.broadcasted_iota(jnp.int32, (2 * CH, 128), 1)

    def pool(a, b):
        lo = lane - jnp.concatenate([sb[a], sb[b]], axis=0)
        hi = lane - jnp.concatenate([eb[a], eb[b]], axis=0)
        total = jnp.zeros((2 * CH, slot), F32)
        wide = 512
        for r in range(0, n_rows, wide):
            tiles = [
                jnp.where((lo >= -(r + t)) & (hi < -(r + t)), 1.0, 0.0).astype(BF)
                for t in range(0, wide, 128)
            ]
            total += dot(jnp.concatenate(tiles, axis=1), nr[0, 0, r : r + wide, :], NN)
        got = jnp.where(keep, total, 0.0).astype(BF)
        pooled[a] = got[:CH]
        pooled[b] = got[CH:]
        return factor * dot(got, npj[0], NN)

    rs = {}

    def reduce_step(step):
        a, b = zz(LONG - step), zz(step - SHORT)
        term = pool(a, b)
        one, two = term[:CH], term[CH:]
        if step > 0:
            rs[True, step - 1].wait_recv()
            one = one + rs_in[step - 1].astype(F32)
        rs_out[step] = one.astype(BF)
        rs[True, step] = send(rs_out.at[step], rs_in.at[step], R_Z + step, tab=zz(1) * NY + y)
        if step > 0:
            rs[False, step - 1].wait_recv()
            two = two + rs_in[LONG + step - 1].astype(F32)
        if step < SHORT:
            rs_out[LONG + step] = two.astype(BF)
            rs[False, step] = send(
                rs_out.at[LONG + step], rs_in.at[LONG + step], R_Z + LONG + step, tab=zz(-1) * NY + y
            )
        else:
            fz[...] = two

    reduce_step(0)
    ring(1)
    reduce_step(1)

    l_wl.wait()
    n_wide = wl.shape[-1]
    tables = wl.shape[0]
    for w in range(tables):
        wlens = jnp.broadcast_to(wl[w].astype(F32), (128, n_wide)).astype(BF)
        for c in range(n_wide // 128):
            row = lax.broadcasted_iota(jnp.int32, (128, n_wide), 0) + c * 128
            place = lax.broadcasted_iota(jnp.int32, (128, n_wide), 1)
            upto = jnp.where(place <= row, 1.0, 0.0).astype(BF)
            below = jnp.where(place < row, 1.0, 0.0).astype(BF)
            web[w, c] = dot(upto, wlens, NT).astype(jnp.int32)
            wsb[w, c] = dot(below, wlens, NT).astype(jnp.int32)
    ring(2)
    l_wr.wait()
    l_wp.wait()
    w_rows = wr.shape[3]
    w_dim = wr.shape[2]
    wlane = lax.broadcasted_iota(jnp.int32, (128, 128), 1)
    parts = []
    for w in range(tables):
        for c in range(n_wide // 128):
            lo = wlane - wsb[w, c]
            hi = wlane - web[w, c]
            for t in range(0, w_rows, 128):
                mask[w, c * 128 : (c + 1) * 128, t : t + 128] = jnp.where(
                    (lo >= -t) & (hi < -t), 1.0, 0.0
                ).astype(BF)
        parts.append(dot(mask[w], wr[w, 0], NT))
    wpooled[...] = jnp.concatenate(parts, axis=1).astype(BF)
    proj = wp[...].reshape(tables * w_dim, wp.shape[2])
    term = (factor * dot(wpooled[...], proj, NN)).astype(BF)
    wterm[...] = term.reshape(wterm.shape)
    ws = send(wterm.at[:, 1 - core], wsib, W_S, col=x * NC + 1 - core)

    ring(3)
    reduce_step(2)

    ws.wait_recv()
    wx_out[...] = (wterm[:, core].astype(F32) + wsib[...].astype(F32)).astype(BF)
    wx = [None]
    for k in range(1, NX):
        p = lax.rem(x + k, NX)
        wx.append(send(wx_out.at[p], wx_in.at[x], W_X + k, col=p * NC + core))
    wx_in[x] = wx_out[x]

    for k in range(1, NX):
        xa[k].wait_recv()
    xs = send(cw.at[:, core], cw.at[:, core], X_S, col=x * NC + 1 - core)

    ring(4)
    reduce_step(3)

    def back_pair(a, b, first, last):
        both = jnp.concatenate([ag[a].reshape(CH, -1), ag[b].reshape(CH, -1)], axis=0)
        back = jnp.where(keep, factor * dot(both, npj[0], NT), 0.0).astype(BF)
        grads = dot(jnp.concatenate([pooled[a], pooled[b]], axis=0), both, TN)
        if first:
            ng_acc[...] = grads
        elif not last:
            ng_acc[...] += grads
        else:
            grads = (factor * (ng_acc[...] + grads)).T
            ng_out[...] = grads.astype(BF).reshape(ng_out.shape)
            for k in range(1, NX):
                p = lax.rem(x + k, NX)
                nx.append(send(ng_out.at[p], ng_in.at[x], N_X + k, col=p * NC + core))
            ng_in[x] = ng_out[x]
        sub = lax.broadcasted_iota(jnp.int32, (8, 2 * CH), 0)
        lo = sub - jnp.concatenate([sr[a][:8], sr[b][:8]], axis=1)
        hi = sub - jnp.concatenate([er[a][:8], er[b][:8]], axis=1)
        deep = 512
        for r in range(0, n_rows, deep):
            rows = jnp.concatenate(
                [
                    jnp.where((lo >= -(r + g)) & (hi < -(r + g)), 1.0, 0.0)
                    for g in range(0, deep, 8)
                ],
                axis=0,
            ).astype(BF)
            got = dot(rows, back, NN)
            if not first:
                got = got + nrg[r : r + deep, :].astype(F32)
            nrg[r : r + deep, :] = got.astype(BF)
            if last:
                c = pltpu.make_async_copy(
                    nrg.at[r : r + deep], o_nr.at[0, 0, r : r + deep], osem.at[r // deep]
                )
                c.start()
                stores.append(c)

    nx = [None]
    stores = []
    back_pair(zz(-1), zz(1), True, False)
    back_pair(zz(-2), zz(2), False, False)

    xs.wait_recv()
    cols = cw[...].reshape(n_wide, -1)
    wback = (factor * dot(proj, cols, NT)).astype(BF)
    wgrads = (factor * dot(wpooled[...], cols, TN)).T
    wg_out[...] = wgrads.astype(BF).reshape(wg_out.shape)
    gz = [None]
    for k in range(1, NZ):
        p = lax.rem(z + k, NZ)
        gz.append(send(wg_out.at[p], wg_in.at[z], G_Z + k, tab=p * NY + y))
    wg_in[z] = wg_out[z]
    for w in range(tables):
        wrg[w, 0] = dot(wback[w * w_dim : (w + 1) * w_dim], mask[w], NN).astype(BF)
        c = pltpu.make_async_copy(wrg.at[w], o_wr.at[w], osem.at[8 + w])
        c.start()
        stores.append(c)

    rs[True, LONG - 1].wait_recv()
    full = fz[...] + rs_in[LONG - 1].astype(F32)
    fz[...] = full
    fy_out[...] = full.astype(BF).reshape(fy_out.shape)
    fy = [None]
    for k in range(1, NY):
        p = lax.rem(y + k, NY)
        fy.append(send(fy_out.at[p], fy_in.at[y], F_Y + k, tab=z * NY + p))
    fy_in[y] = jnp.zeros(fy_in.shape[1:], BF)

    back_pair(zz(-3), zz(3), False, False)

    for k in range(1, NZ):
        gz[k].wait_recv()
    wsum = jnp.sum(wg_in[...].astype(F32), axis=0)
    wg2_out[...] = wsum.reshape(wg2_out.shape)
    gy = [None]
    for k in range(1, NYF):
        p = lax.rem(yf + k, NYF)
        gy.append(
            send(wg2_out.at[p], wg2_in.at[yf], G_Y + k, tab=z * NY + p // ND, dp=lax.rem(p, ND))
        )
    wg2_in[yf] = wg2_out[yf]

    back_pair(zz(-4), z, False, True)

    for k in range(1, NX):
        nx[k].wait_recv()
    nsum = jnp.sum(ng_in[...].astype(F32), axis=0)
    nq_out[...] = nsum.reshape(nq_out.shape)
    me = core * ND + dp
    nq = [
        send(nq_out.at[(1 - core) * ND + dp], nq_in.at[me], N_Q + 1, col=x * NC + 1 - core),
        send(nq_out.at[core * ND + 1 - dp], nq_in.at[me], N_Q + 2, dp=1 - dp),
        send(
            nq_out.at[(1 - core) * ND + 1 - dp], nq_in.at[me], N_Q + 3,
            col=x * NC + 1 - core, dp=1 - dp,
        ),
    ]
    nq_in[me] = nq_out[me]

    for k in range(1, NY):
        fy[k].wait_recv()
    for k in range(1, NX):
        wx[k].wait_recv()
    total = fz[pl.ds(pl.multiple_of(y * PER, PER), PER), :]
    total = total + jnp.sum(fy_in[...].astype(F32), axis=0) + jnp.sum(wx_in[...].astype(F32), axis=0)
    xo[...] = total.astype(BF)
    c = pltpu.make_async_copy(xo, o_x, osem.at[10])
    c.start()
    stores.append(c)

    for k in range(1, NYF):
        gy[k].wait_recv()
    wout = jnp.sum(wg2_in[...], axis=0)
    for w in range(tables):
        wgo[w] = wout[:, w * w_dim : (w + 1) * w_dim]
    c = pltpu.make_async_copy(wgo, o_wg, osem.at[11])
    c.start()
    stores.append(c)

    for c in nq:
        c.wait_recv()
    ngo[0] = jnp.sum(nq_in[...], axis=0)
    c = pltpu.make_async_copy(ngo, o_ng, osem.at[12])
    c.start()
    stores.append(c)

    for c in sent:
        c.wait_send()
    for c in stores:
        c.wait()


def body(
    wide_rows,
    wide_lengths,
    narrow_rows,
    narrow_lengths,
    narrow_widths,
    wide_proj,
    narrow_proj,
    cotangent,
):
    out_width = cotangent.shape[1]
    tables, _, w_rows, w_dim = wide_rows.shape
    n_rows, slot = narrow_rows.shape[2:]
    n_wide, n_narrow = wide_lengths.shape[2], narrow_lengths.shape[2]
    factor = (tables + narrow_rows.shape[0] * lax.axis_size("tab")) ** (-0.5)
    rows_t = jnp.transpose(wide_rows, (0, 1, 3, 2))
    wk = tables * w_dim
    v = pltpu.VMEM
    scratch = [
        v((tables, 1, w_dim, w_rows), BF), v(wide_lengths.shape, jnp.int32),
        v(narrow_rows.shape, BF), v(narrow_lengths.shape, jnp.int32),
        v(wide_proj.shape, BF), v(narrow_proj.shape, BF), v(cotangent.shape, BF),
        v((NZ, CH, 128), jnp.int32), v((NZ, CH, 128), jnp.int32),
        v((NZ, 16, 128), jnp.int32), v((NZ, 16, 128), jnp.int32),
        v((tables, n_wide // 128, 128, 128), jnp.int32), v((tables, n_wide // 128, 128, 128), jnp.int32),
        v((NZ, CH, slot), BF), v((tables, n_wide, w_rows), BF), v((n_wide, wk), BF),
        v((NX, NC, PER, out_width), BF), v((NZ, NY, PER, out_width), BF), v((NX, NC, PER, out_width), BF),
        v((LONG + SHORT, CH, out_width), BF), v((LONG + SHORT, CH, out_width), BF),
        v((NX, PER, out_width), BF), v((NX, PER, out_width), BF), v((NX, PER, out_width), BF),
        v((CH, out_width), F32), v((NY, PER, out_width), BF), v((NY, PER, out_width), BF),
        v((NZ, out_width // NZ, wk), BF), v((NZ, out_width // NZ, wk), BF),
        v((NYF, out_width // NZ // NYF, wk), F32), v((NYF, out_width // NZ // NYF, wk), F32),
        v((slot, out_width), F32), v((NX, out_width // NX, slot), BF), v((NX, out_width // NX, slot), BF),
        v((NC * ND, out_width // NX // NC // ND, slot), F32), v((NC * ND, out_width // NX // NC // ND, slot), F32),
        v((n_rows, slot), BF), v((tables, 1, w_dim, w_rows), BF), v((PER, out_width), BF),
        v((tables, out_width // NZ // NYF, w_dim), F32), v((1, out_width // NX // NC // ND, slot), F32),
        pltpu.SemaphoreType.DMA((N_SEM,)), pltpu.SemaphoreType.DMA((N_SEM,)),
        pltpu.SemaphoreType.DMA((8,)), pltpu.SemaphoreType.DMA((16,)),
    ]
    hbm = pl.BlockSpec(memory_space=pl.ANY)
    smem = pl.BlockSpec(memory_space=pltpu.SMEM)
    s = jax.ShapeDtypeStruct
    outs = pl.pallas_call(
        functools.partial(kernel, factor),
        name="sparse_arch",
        out_shape=(
            s((PER, out_width), BF),
            s((tables, 1, w_dim, w_rows), BF),
            s(narrow_rows.shape, BF),
            s((tables, out_width // NZ // NYF, w_dim), F32),
            s((1, out_width // NX // NC // ND, slot), F32),
        ),
        in_specs=[hbm, hbm, hbm, hbm, smem, hbm, hbm, hbm],
        out_specs=(hbm,) * 5,
        scratch_shapes=scratch,
        compiler_params=pltpu.CompilerParams(
            collective_id=0, has_side_effects=True, vmem_limit_bytes=48 * 1024 * 1024
        ),
    )(rows_t, wide_lengths, narrow_rows, narrow_lengths, narrow_widths, wide_proj, narrow_proj, cotangent)
    cross, wide_t, narrow, wide_g, narrow_g = outs
    return (
        cross,
        jnp.transpose(wide_t, (0, 1, 3, 2)),
        narrow,
        jnp.transpose(wide_g, (0, 2, 1)),
        jnp.transpose(narrow_g, (0, 2, 1)),
    )


def solution(mesh):
    in_specs = (
        P(None, ("tab", "dp"), None, "col"),
        P(None, ("tab", "dp"), None),
        P("tab", ("col", "dp"), None, None),
        P("tab", ("col", "dp"), None),
        P("tab"),
        P(None, "col", None),
        P("tab", None, None),
        P(("col", "tab", "dp"), None),
    )
    out_specs = (
        P(("col", "tab", "dp"), None),
        P(None, ("tab", "dp"), None, "col"),
        P("tab", ("col", "dp"), None, None),
        P(None, "col", ("tab", "dp")),
        P("tab", None, ("col", "dp")),
    )
    return jax.shard_map(body, mesh=mesh, in_specs=in_specs, out_specs=out_specs, check_vma=False)
```

```python
import functools

import jax
import jax.numpy as jnp
from jax import lax
from jax.experimental import pallas as pl
from jax.experimental.pallas import tpu as pltpu
from jax.sharding import PartitionSpec as P

MESH = pl.DeviceIdType.MESH
BF = jnp.bfloat16
F32 = jnp.float32

NX, NC, NZ, NY, ND = 8, 2, 8, 4, 2
NYF = NY * ND
VMEM = 56 * 1024 * 1024
PER = 32
CH = NY * PER
LONG, SHORT = 4, 3

NT = (((1,), (1,)), ((), ()))
TN = (((0,), (0,)), ((), ()))
NN = (((1,), (0,)), ((), ()))

A_Y = 0
A_Z = A_Y + NY
R_Z = A_Z + 2 * LONG * NY
X_A = R_Z + 2 * LONG * NY
X_S = X_A + NX
W_S = X_S + 1
W_X = W_S + 1
F_Y = W_X + NX
G_Z = F_Y + NY * NY
G_Y = G_Z + LONG + SHORT
N_X = G_Y + NYF
N_Q = N_X + NX
N_SEM = N_Q + NC * ND


def dot(a, b, dims):
    return lax.dot_general(a, b, dims, preferred_element_type=F32)


def kernel(
    factor,
    wr_h, wl_h, nr_h, nl_h, nw, wp_h, np_h, cot_h,
    o_x, o_wr, o_nr, o_wg, o_ng,
    wr, wl, nr, nl, wp, npj, cot,
    sb, eb, sr, er, wsb, web,
    pooled, mask, wpooled, wterm, ag, cw,
    rs_out, rs_in, wsib, wx_out, wx_in, fz, fy_out, fy_in,
    wg, wgz, wg_out, wg_in, wg2_out, wg2_in, ng_acc, ng_out, ng_in, nq_out, nq_in,
    back, nrg, wrg, xo, wgo, ngo,
    snd, rcv, isem, osem,
):
    col, tab, dp = lax.axis_index("col"), lax.axis_index("tab"), lax.axis_index("dp")
    x, core = col // NC, lax.rem(col, NC)
    z, y = tab // NY, lax.rem(tab, NY)
    yf = y * ND + dp
    sgn = 1 - 2 * core

    def zz(k):
        return lax.rem(z + sgn * k + 4 * NZ, NZ)

    bar = pltpu.get_barrier_semaphore()

    def hello(**dev):
        pl.semaphore_signal(bar, inc=1, device_id=dev, device_id_type=MESH)

    for k in range(1, NYF):
        p = lax.rem(yf + k, NYF)
        hello(tab=z * NY + p // ND, dp=lax.rem(p, ND))
    for k in (1, NZ - 1):
        hello(tab=lax.rem(z + k, NZ) * NY + y)
    for k in range(1, NX):
        hello(col=lax.rem(x + k, NX) * NC + core)
    hello(col=x * NC + 1 - core)
    hello(col=x * NC + 1 - core, dp=1 - dp)

    loads = [
        pltpu.make_async_copy(s, d, isem.at[i])
        for i, (s, d) in enumerate(
            [(cot_h, cot), (nl_h, nl), (nr_h, nr), (np_h, npj), (wl_h, wl), (wr_h, wr), (wp_h, wp)]
        )
    ]
    for c in loads:
        c.start()
    l_cot, l_nl, l_nr, l_np, l_wl, l_wr, l_wp = loads

    sent, stores = [], []

    def keep_out(src, dst):
        c = pltpu.make_async_copy(src, dst, osem.at[len(stores)])
        c.start()
        stores.append(c)


    def copy(src, dst, i, **dev):
        return pltpu.make_async_remote_copy(
            src_ref=src, dst_ref=dst, send_sem=snd.at[i], recv_sem=rcv.at[i],
            device_id=dev, device_id_type=MESH,
        )

    def send(*args, **dev):
        c = copy(*args, **dev)
        c.start()
        sent.append(c)
        return c

    l_cot.wait()
    pl.semaphore_wait(bar, (NYF - 1) + 2 + (NX - 1) + 2)

    ay = [None]
    for k in range(1, NY):
        p = lax.rem(y + k, NY)
        ay.append(send(cot, ag.at[z, y], A_Y + k, tab=z * NY + p))
    ag[z, y] = cot[...]
    cw[x, core] = cot[...]

    az = {}

    def forward(step, k):
        q = lax.rem(y - k + NY, NY)
        if step < LONG:
            b = zz(-step)
            az[True, step, k] = send(
                ag.at[b, q], ag.at[b, q], A_Z + step * NY + k, tab=zz(1) * NY + y
            )
        if step < SHORT:
            b = zz(step)
            az[False, step, k] = send(
                ag.at[b, q], ag.at[b, q], A_Z + (LONG + step) * NY + k, tab=zz(-1) * NY + y
            )

    def ring(step, k):
        az[True, step - 1, k].wait_recv()
        if step - 1 < SHORT:
            az[False, step - 1, k].wait_recv()
        if step < LONG:
            forward(step, k)

    forward(0, 0)
    xa = [None]
    for k in range(1, NX):
        p = lax.rem(x + k, NX)
        xa.append(send(cot, cw.at[x, core], X_A + k, col=p * NC + core))

    l_nl.wait()
    n_narrow = nl.shape[-1]
    lens = jnp.broadcast_to(nl[0].astype(F32), (CH, n_narrow)).astype(BF)
    for c in range(n_narrow // CH):
        row = lax.broadcasted_iota(jnp.int32, (CH, n_narrow), 0) + c * CH
        place = lax.broadcasted_iota(jnp.int32, (CH, n_narrow), 1)
        upto = jnp.where(place <= row, 1.0, 0.0).astype(BF)
        below = jnp.where(place < row, 1.0, 0.0).astype(BF)
        eb[c] = dot(upto, lens, NT).astype(jnp.int32)
        sb[c] = dot(below, lens, NT).astype(jnp.int32)
        er[c] = dot(lens[:16], upto, NT).astype(jnp.int32)
        sr[c] = dot(lens[:16], below, NT).astype(jnp.int32)

    for k in range(1, NY):
        ay[k].wait_recv()
        forward(0, k)

    l_np.wait()
    l_nr.wait()
    n_rows = nr.shape[2]
    slot = nr.shape[3]
    keep = lax.broadcasted_iota(jnp.int32, (2 * CH, slot), 1) < nw[0]
    lane = lax.broadcasted_iota(jnp.int32, (2 * CH, 128), 1)

    def pool(a, b):
        lo = lane - jnp.concatenate([sb[a], sb[b]], axis=0)
        hi = lane - jnp.concatenate([eb[a], eb[b]], axis=0)
        total = jnp.zeros((2 * CH, slot), F32)
        wide = 512
        for r in range(0, n_rows, wide):
            tiles = [
                jnp.where((lo >= -(r + t)) & (hi < -(r + t)), 1.0, 0.0).astype(BF)
                for t in range(0, wide, 128)
            ]
            total += dot(jnp.concatenate(tiles, axis=1), nr[0, 0, r : r + wide, :], NN)
        got = jnp.where(keep, total, 0.0).astype(BF)
        pooled[a] = got[:CH]
        pooled[b] = got[CH:]
        return factor * dot(got, npj[0], NN)

    rs = {}

    def reduce_long(step, q, mine):
        if step > 0:
            rs[True, step - 1, q].wait_recv()
            mine = mine + rs_in[step - 1, q].astype(F32)
        rs_out[step, q] = mine.astype(BF)
        rs[True, step, q] = send(
            rs_out.at[step, q], rs_in.at[step, q], R_Z + step * NY + q, tab=zz(1) * NY + y
        )

    def reduce_short(step, q, mine):
        if step > 0:
            rs[False, step - 1, q].wait_recv()
            mine = mine + rs_in[LONG + step - 1, q].astype(F32)
        if step < SHORT:
            rs_out[LONG + step, q] = mine.astype(BF)
            rs[False, step, q] = send(
                rs_out.at[LONG + step, q], rs_in.at[LONG + step, q],
                R_Z + (LONG + step) * NY + q, tab=zz(-1) * NY + y,
            )
        else:
            fz[q] = mine

    def reduce_step(step, term):
        for q in range(NY):
            reduce_long(step, q, term[q * PER : (q + 1) * PER])
            reduce_short(step, q, term[CH + q * PER : CH + (q + 1) * PER])

    def gather_step(step):
        for k in range(NY):
            ring(step, k)

    term = pool(zz(LONG), zz(-SHORT))
    reduce_step(0, term)
    term = pool(zz(LONG - 1), zz(1 - SHORT))
    gather_step(1)
    reduce_step(1, term)

    l_wl.wait()
    n_wide = wl.shape[-1]
    tables = wl.shape[0]
    for w in range(tables):
        wlens = jnp.broadcast_to(wl[w].astype(F32), (128, n_wide)).astype(BF)
        for c in range(n_wide // 128):
            row = lax.broadcasted_iota(jnp.int32, (128, n_wide), 0) + c * 128
            place = lax.broadcasted_iota(jnp.int32, (128, n_wide), 1)
            upto = jnp.where(place <= row, 1.0, 0.0).astype(BF)
            below = jnp.where(place < row, 1.0, 0.0).astype(BF)
            web[w, c] = dot(upto, wlens, NT).astype(jnp.int32)
            wsb[w, c] = dot(below, wlens, NT).astype(jnp.int32)
    l_wr.wait()
    l_wp.wait()
    w_rows = wr.shape[3]
    w_dim = wr.shape[2]
    wlane = lax.broadcasted_iota(jnp.int32, (128, 128), 1)
    parts = []
    for w in range(tables):
        for c in range(n_wide // 128):
            lo = wlane - wsb[w, c]
            hi = wlane - web[w, c]
            for t in range(0, w_rows, 128):
                mask[w, c * 128 : (c + 1) * 128, t : t + 128] = jnp.where(
                    (lo >= -t) & (hi < -t), 1.0, 0.0
                ).astype(BF)
        parts.append(dot(mask[w], wr[w, 0], NT))
    wpooled[...] = jnp.concatenate(parts, axis=1).astype(BF)
    proj = wp[...].reshape(tables * w_dim, wp.shape[2])
    term = (factor * dot(wpooled[...], proj, NN)).astype(BF)
    wterm[...] = term.reshape(wterm.shape)
    ws = send(wterm.at[:, 1 - core], wsib, W_S, col=x * NC + 1 - core)
    for k in range(1, NX):
        xa[k].wait_recv()
    xs = send(cw.at[:, core], cw.at[:, core], X_S, col=x * NC + 1 - core)

    def grads_pair(a, b, i):
        both = jnp.concatenate([ag[a].reshape(CH, -1), ag[b].reshape(CH, -1)], axis=0)
        back[i] = jnp.where(keep, factor * dot(both, npj[0], NT), 0.0).astype(BF)
        grads = dot(jnp.concatenate([pooled[a], pooled[b]], axis=0), both, TN)
        if i == 0:
            ng_acc[...] = grads
        else:
            ng_acc[...] += grads

    def rows_pair(a, b, i):
        sub = lax.broadcasted_iota(jnp.int32, (8, 2 * CH), 0)
        lo = sub - jnp.concatenate([sr[a][:8], sr[b][:8]], axis=1)
        hi = sub - jnp.concatenate([er[a][:8], er[b][:8]], axis=1)
        deep = 512
        for r in range(0, n_rows, deep):
            rows = jnp.concatenate(
                [
                    jnp.where((lo >= -(r + g)) & (hi < -(r + g)), 1.0, 0.0)
                    for g in range(0, deep, 8)
                ],
                axis=0,
            ).astype(BF)
            got = dot(rows, back[i], NN)
            if i > 0:
                got = got + nrg[r : r + deep, :].astype(F32)
            nrg[r : r + deep, :] = got.astype(BF)
            if i == LONG - 1:
                keep_out(nrg.at[r : r + deep], o_nr.at[0, 0, r : r + deep])

    gr = {}

    def wide_step(step):
        one, two = wg[zz(LONG - step)], wg[zz(step - SHORT)]
        if step > 0:
            gr[True, step - 1].wait_recv()
            one = one + wg_in[step - 1].astype(F32)
            gr[False, step - 1].wait_recv()
            two = two + wg_in[LONG + step - 1].astype(F32)
        wg_out[step] = one.astype(BF)
        gr[True, step] = send(wg_out.at[step], wg_in.at[step], G_Z + step, tab=zz(1) * NY + y)
        if step < SHORT:
            wg_out[LONG + step] = two.astype(BF)
            gr[False, step] = send(
                wg_out.at[LONG + step], wg_in.at[LONG + step], G_Z + LONG + step, tab=zz(-1) * NY + y
            )
        else:
            wgz[...] = two

    term = pool(zz(LONG - 2), zz(2 - SHORT))
    gather_step(2)
    reduce_step(2, term)

    ws.wait_recv()
    wx_out[...] = (wterm[:, core].astype(F32) + wsib[...].astype(F32)).astype(BF)
    wx = [None]
    for k in range(1, NX):
        p = lax.rem(x + k, NX)
        wx.append(send(wx_out.at[p], wx_in.at[x], W_X + k, col=p * NC + core))
    wx_in[x] = wx_out[x]

    xs.wait_recv()
    cols = cw[...].reshape(n_wide, -1)
    wg[...] = (factor * dot(wpooled[...], cols, TN)).T.reshape(wg.shape)
    wide_step(0)

    term = pool(zz(LONG - 3), z)
    grads_pair(zz(-1), zz(1), 0)
    rows_pair(zz(-1), zz(1), 0)
    gather_step(3)
    reduce_step(3, term)
    wide_step(1)

    grads_pair(zz(-2), zz(2), 1)
    grads_pair(zz(-3), zz(3), 2)
    rows_pair(zz(-2), zz(2), 1)

    gather_step(LONG)
    grads_pair(zz(-4), z, 3)
    ng_out[...] = (factor * ng_acc[...]).T.astype(BF).reshape(ng_out.shape)
    nx = [None]
    for k in range(1, NX):
        p = lax.rem(x + k, NX)
        nx.append(send(ng_out.at[p], ng_in.at[x], N_X + k, col=p * NC + core))
    ng_in[x] = ng_out[x]
    wide_step(2)

    rows_pair(zz(-3), zz(3), 2)

    for q in range(NY):
        rs[True, LONG - 1, q].wait_recv()
        full = fz[q] + rs_in[LONG - 1, q].astype(F32)
        fz[q] = full
        fy_out[q] = full.astype(BF)

        @pl.when(y != q)
        def _():
            copy(fy_out.at[q], fy_in.at[y], F_Y + q * NY + y, tab=z * NY + q).start()

    fy_in[y] = jnp.zeros(fy_in.shape[1:], BF)
    wide_step(3)

    for k in range(1, NX):
        nx[k].wait_recv()
    nsum = jnp.sum(ng_in[...].astype(F32), axis=0)
    nq_out[...] = nsum.reshape(nq_out.shape)
    me = core * ND + dp
    nq = [
        send(nq_out.at[(1 - core) * ND + dp], nq_in.at[me], N_Q + 1, col=x * NC + 1 - core),
        send(nq_out.at[core * ND + 1 - dp], nq_in.at[me], N_Q + 2, dp=1 - dp),
        send(
            nq_out.at[(1 - core) * ND + 1 - dp], nq_in.at[me], N_Q + 3,
            col=x * NC + 1 - core, dp=1 - dp,
        ),
    ]
    nq_in[me] = nq_out[me]

    wback = (factor * dot(proj, cw[...].reshape(n_wide, -1), NT)).astype(BF)
    for w in range(tables):
        wrg[w, 0] = dot(wback[w * w_dim : (w + 1) * w_dim], mask[w], NN).astype(BF)
        keep_out(wrg.at[w], o_wr.at[w])

    gr[True, LONG - 1].wait_recv()
    wsum = wgz[...] + wg_in[LONG - 1].astype(F32)
    wg2_out[...] = wsum.reshape(wg2_out.shape)
    gy = [None]
    for k in range(1, NYF):
        p = lax.rem(yf + k, NYF)
        gy.append(
            send(wg2_out.at[p], wg2_in.at[yf], G_Y + k, tab=z * NY + p // ND, dp=lax.rem(p, ND))
        )
    wg2_in[yf] = wg2_out[yf]

    rows_pair(zz(-4), z, 3)

    for k in range(1, NY):
        p = lax.rem(y + k, NY)
        copy(fy_out.at[p], fy_in.at[p], F_Y + y * NY + p, tab=z * NY + p).wait_recv()
        copy(fy_out.at[p], fy_in.at[y], F_Y + p * NY + y, tab=z * NY + p).wait_send()
    for k in range(1, NX):
        wx[k].wait_recv()
    total = fz[y] + jnp.sum(fy_in[...].astype(F32), axis=0) + jnp.sum(wx_in[...].astype(F32), axis=0)
    xo[...] = total.astype(BF)
    keep_out(xo, o_x)

    for k in range(1, NYF):
        gy[k].wait_recv()
    wout = jnp.sum(wg2_in[...], axis=0)
    for w in range(tables):
        wgo[w] = wout[:, w * w_dim : (w + 1) * w_dim]
    keep_out(wgo, o_wg)

    for c in nq:
        c.wait_recv()
    ngo[0] = jnp.sum(nq_in[...], axis=0)
    keep_out(ngo, o_ng)

    for c in sent:
        c.wait_send()
    for c in stores:
        c.wait()


def store(*refs):
    n = len(refs) // 3
    src, dst, held, sem = refs[:n], refs[n : 2 * n], refs[2 * n : 3 * n], refs[3 * n]
    order = sorted(range(n), key=lambda i: -src[i].size)
    come = {i: pltpu.make_async_copy(src[i], held[i], sem.at[i]) for i in order}
    go = {i: pltpu.make_async_copy(held[i], dst[i], sem.at[n + i]) for i in order}
    for i in order:
        come[i].start()
    for i in reversed(order):
        come[i].wait()
        go[i].start()
    for i in order:
        go[i].wait()


def body(
    wide_rows,
    wide_lengths,
    narrow_rows,
    narrow_lengths,
    narrow_widths,
    wide_proj,
    narrow_proj,
    cotangent,
):
    out_width = cotangent.shape[1]
    tables, _, w_rows, w_dim = wide_rows.shape
    n_rows, slot = narrow_rows.shape[2:]
    n_wide, n_narrow = wide_lengths.shape[2], narrow_lengths.shape[2]
    factor = (tables + narrow_rows.shape[0] * lax.axis_size("tab")) ** (-0.5)
    rows_t = jnp.transpose(wide_rows, (0, 1, 3, 2))
    wk = tables * w_dim
    v = pltpu.VMEM
    scratch = [
        v((tables, 1, w_dim, w_rows), BF), v(wide_lengths.shape, jnp.int32),
        v(narrow_rows.shape, BF), v(narrow_lengths.shape, jnp.int32),
        v(wide_proj.shape, BF), v(narrow_proj.shape, BF), v(cotangent.shape, BF),
        v((NZ, CH, 128), jnp.int32), v((NZ, CH, 128), jnp.int32),
        v((NZ, 16, 128), jnp.int32), v((NZ, 16, 128), jnp.int32),
        v((tables, n_wide // 128, 128, 128), jnp.int32), v((tables, n_wide // 128, 128, 128), jnp.int32),
        v((NZ, CH, slot), BF), v((tables, n_wide, w_rows), BF), v((n_wide, wk), BF),
        v((NX, NC, PER, out_width), BF), v((NZ, NY, PER, out_width), BF), v((NX, NC, PER, out_width), BF),
        v((LONG + SHORT, NY, PER, out_width), BF), v((LONG + SHORT, NY, PER, out_width), BF),
        v((NX, PER, out_width), BF), v((NX, PER, out_width), BF), v((NX, PER, out_width), BF),
        v((NY, PER, out_width), F32), v((NY, PER, out_width), BF), v((NY, PER, out_width), BF),
        v((NZ, out_width // NZ, wk), F32), v((out_width // NZ, wk), F32),
        v((LONG + SHORT, out_width // NZ, wk), BF), v((LONG + SHORT, out_width // NZ, wk), BF),
        v((NYF, out_width // NZ // NYF, wk), F32), v((NYF, out_width // NZ // NYF, wk), F32),
        v((slot, out_width), F32), v((NX, out_width // NX, slot), BF), v((NX, out_width // NX, slot), BF),
        v((NC * ND, out_width // NX // NC // ND, slot), F32), v((NC * ND, out_width // NX // NC // ND, slot), F32),
        v((LONG, 2 * CH, slot), BF), v((n_rows, slot), BF), v((tables, 1, w_dim, w_rows), BF), v((PER, out_width), BF),
        v((tables, out_width // NZ // NYF, w_dim), F32), v((1, out_width // NX // NC // ND, slot), F32),
        pltpu.SemaphoreType.DMA((N_SEM,)), pltpu.SemaphoreType.DMA((N_SEM,)),
        pltpu.SemaphoreType.DMA((8,)), pltpu.SemaphoreType.DMA((16,)),
    ]
    hbm = pl.BlockSpec(memory_space=pl.ANY)
    smem = pl.BlockSpec(memory_space=pltpu.SMEM)
    s = jax.ShapeDtypeStruct
    outs = pl.pallas_call(
        functools.partial(kernel, factor),
        name="sparse_arch",
        out_shape=(
            s((PER, out_width), BF),
            s((tables, 1, w_dim, w_rows), BF),
            s(narrow_rows.shape, BF),
            s((tables, out_width // NZ // NYF, w_dim), F32),
            s((1, out_width // NX // NC // ND, slot), F32),
        ),
        in_specs=[hbm, hbm, hbm, hbm, smem, hbm, hbm, hbm],
        out_specs=(hbm,) * 5,
        scratch_shapes=scratch,
        compiler_params=pltpu.CompilerParams(
            collective_id=0, has_side_effects=True, vmem_limit_bytes=VMEM
        ),
    )(rows_t, wide_lengths, narrow_rows, narrow_lengths, narrow_widths, wide_proj, narrow_proj, cotangent)
    cross, wide_t, narrow, wide_g, narrow_g = pl.pallas_call(
        store,
        name="store",
        out_shape=[s(o.shape, o.dtype) for o in outs],
        in_specs=[hbm] * len(outs),
        out_specs=[hbm] * len(outs),
        scratch_shapes=[v(o.shape, o.dtype) for o in outs] + [pltpu.SemaphoreType.DMA((2 * len(outs),))],
        compiler_params=pltpu.CompilerParams(vmem_limit_bytes=VMEM),
    )(*outs)
    return (
        cross,
        jnp.transpose(wide_t, (0, 1, 3, 2)),
        narrow,
        jnp.transpose(wide_g, (0, 2, 1)),
        jnp.transpose(narrow_g, (0, 2, 1)),
    )


def solution(mesh):
    in_specs = (
        P(None, ("tab", "dp"), None, "col"),
        P(None, ("tab", "dp"), None),
        P("tab", ("col", "dp"), None, None),
        P("tab", ("col", "dp"), None),
        P("tab"),
        P(None, "col", None),
        P("tab", None, None),
        P(("col", "tab", "dp"), None),
    )
    out_specs = (
        P(("col", "tab", "dp"), None),
        P(None, ("tab", "dp"), None, "col"),
        P("tab", ("col", "dp"), None, None),
        P(None, "col", ("tab", "dp")),
        P("tab", None, ("col", "dp")),
    )
    return jax.shard_map(body, mesh=mesh, in_specs=in_specs, out_specs=out_specs, check_vma=False)
```

```python
import functools

import jax
import jax.numpy as jnp
from jax import lax
from jax.experimental import pallas as pl
from jax.experimental.pallas import tpu as pltpu
from jax.sharding import PartitionSpec as P

MESH = pl.DeviceIdType.MESH
BF = jnp.bfloat16
F32 = jnp.float32

NX, NC, NZ, NY, ND = 8, 2, 8, 4, 2
NYF = NY * ND
STORE_PARTS = 4
VMEM = 56 * 1024 * 1024
PER = 32
CH = NY * PER
LONG, SHORT = 4, 3

NT = (((1,), (1,)), ((), ()))
TN = (((0,), (0,)), ((), ()))
NN = (((1,), (0,)), ((), ()))

A_Y = 0
A_Z = A_Y + NY
R_Z = A_Z + 2 * LONG * NY
X_A = R_Z + 2 * LONG * NY
X_S = X_A + NX
W_S = X_S + 1
W_X = W_S + 1
F_Y = W_X + NX
G_Z = F_Y + NY * NY
G_Y = G_Z + LONG + SHORT
N_X = G_Y + NYF
N_Q = N_X + NX
N_SEM = N_Q + NC * ND


def dot(a, b, dims):
    return lax.dot_general(a, b, dims, preferred_element_type=F32)


def kernel(
    factor,
    wr_h, wl_h, nr_h, nl_h, nw, wp_h, np_h, cot_h,
    o_x, o_wr, o_nr, o_wg, o_ng,
    wr, wl, nr, nl, wp, npj, cot,
    sb, eb, sr, er, wsb, web,
    pooled, mask, wpooled, wterm, ag, cw,
    rs_out, rs_in, wsib, wx_out, wx_in, fz, fy_out, fy_in,
    wg, wgz, wg_out, wg_in, wg2_out, wg2_in, ng_acc, ng_out, ng_in, nq_out, nq_in,
    back, nrg, wrg, xo, wgo, ngo,
    snd, rcv, isem, osem,
):
    col, tab, dp = lax.axis_index("col"), lax.axis_index("tab"), lax.axis_index("dp")
    x, core = col // NC, lax.rem(col, NC)
    z, y = tab // NY, lax.rem(tab, NY)
    yf = y * ND + dp
    sgn = 1 - 2 * core

    def zz(k):
        return lax.rem(z + sgn * k + 4 * NZ, NZ)

    bar = pltpu.get_barrier_semaphore()

    def hello(**dev):
        pl.semaphore_signal(bar, inc=1, device_id=dev, device_id_type=MESH)

    for k in range(1, NYF):
        p = lax.rem(yf + k, NYF)
        hello(tab=z * NY + p // ND, dp=lax.rem(p, ND))
    for k in (1, NZ - 1):
        hello(tab=lax.rem(z + k, NZ) * NY + y)
    for k in range(1, NX):
        hello(col=lax.rem(x + k, NX) * NC + core)
    hello(col=x * NC + 1 - core)
    hello(col=x * NC + 1 - core, dp=1 - dp)

    loads = [
        pltpu.make_async_copy(s, d, isem.at[i])
        for i, (s, d) in enumerate(
            [(cot_h, cot), (nl_h, nl), (nr_h, nr), (np_h, npj), (wl_h, wl), (wr_h, wr), (wp_h, wp)]
        )
    ]
    for c in loads:
        c.start()
    l_cot, l_nl, l_nr, l_np, l_wl, l_wr, l_wp = loads

    sent, stores = [], []

    def keep_out(src, dst):
        c = pltpu.make_async_copy(src, dst, osem.at[len(stores)])
        c.start()
        stores.append(c)


    def copy(src, dst, i, **dev):
        return pltpu.make_async_remote_copy(
            src_ref=src, dst_ref=dst, send_sem=snd.at[i], recv_sem=rcv.at[i],
            device_id=dev, device_id_type=MESH,
        )

    def send(*args, **dev):
        c = copy(*args, **dev)
        c.start()
        sent.append(c)
        return c

    l_cot.wait()
    pl.semaphore_wait(bar, (NYF - 1) + 2 + (NX - 1) + 2)

    ay = [None]
    for k in range(1, NY):
        p = lax.rem(y + k, NY)
        ay.append(send(cot, ag.at[z, y], A_Y + k, tab=z * NY + p))
    ag[z, y] = cot[...]
    cw[x, core] = cot[...]

    az = {}

    def forward(step, k):
        q = lax.rem(y - k + NY, NY)
        if step < LONG:
            b = zz(-step)
            az[True, step, k] = send(
                ag.at[b, q], ag.at[b, q], A_Z + step * NY + k, tab=zz(1) * NY + y
            )
        if step < SHORT:
            b = zz(step)
            az[False, step, k] = send(
                ag.at[b, q], ag.at[b, q], A_Z + (LONG + step) * NY + k, tab=zz(-1) * NY + y
            )

    def ring(step, k):
        az[True, step - 1, k].wait_recv()
        if step - 1 < SHORT:
            az[False, step - 1, k].wait_recv()
        if step < LONG:
            forward(step, k)

    forward(0, 0)
    xa = [None]
    for k in range(1, NX):
        p = lax.rem(x + k, NX)
        xa.append(send(cot, cw.at[x, core], X_A + k, col=p * NC + core))

    l_nl.wait()
    n_narrow = nl.shape[-1]
    lens = jnp.broadcast_to(nl[0].astype(F32), (CH, n_narrow)).astype(BF)
    for c in range(n_narrow // CH):
        row = lax.broadcasted_iota(jnp.int32, (CH, n_narrow), 0) + c * CH
        place = lax.broadcasted_iota(jnp.int32, (CH, n_narrow), 1)
        upto = jnp.where(place <= row, 1.0, 0.0).astype(BF)
        below = jnp.where(place < row, 1.0, 0.0).astype(BF)
        eb[c] = dot(upto, lens, NT).astype(jnp.int32)
        sb[c] = dot(below, lens, NT).astype(jnp.int32)
        er[c] = dot(lens[:16], upto, NT).astype(jnp.int32)
        sr[c] = dot(lens[:16], below, NT).astype(jnp.int32)

    for k in range(1, NY):
        ay[k].wait_recv()
        forward(0, k)

    l_np.wait()
    l_nr.wait()
    n_rows = nr.shape[2]
    slot = nr.shape[3]
    keep = lax.broadcasted_iota(jnp.int32, (2 * CH, slot), 1) < nw[0]
    lane = lax.broadcasted_iota(jnp.int32, (2 * CH, 128), 1)

    def pool(a, b):
        lo = lane - jnp.concatenate([sb[a], sb[b]], axis=0)
        hi = lane - jnp.concatenate([eb[a], eb[b]], axis=0)
        total = jnp.zeros((2 * CH, slot), F32)
        wide = 512
        for r in range(0, n_rows, wide):
            tiles = [
                jnp.where((lo >= -(r + t)) & (hi < -(r + t)), 1.0, 0.0).astype(BF)
                for t in range(0, wide, 128)
            ]
            total += dot(jnp.concatenate(tiles, axis=1), nr[0, 0, r : r + wide, :], NN)
        got = jnp.where(keep, total, 0.0).astype(BF)
        pooled[a] = got[:CH]
        pooled[b] = got[CH:]
        return factor * dot(got, npj[0], NN)

    rs = {}

    def reduce_long(step, q, mine):
        if step > 0:
            rs[True, step - 1, q].wait_recv()
            mine = mine + rs_in[step - 1, q].astype(F32)
        rs_out[step, q] = mine.astype(BF)
        rs[True, step, q] = send(
            rs_out.at[step, q], rs_in.at[step, q], R_Z + step * NY + q, tab=zz(1) * NY + y
        )

    def reduce_short(step, q, mine):
        if step > 0:
            rs[False, step - 1, q].wait_recv()
            mine = mine + rs_in[LONG + step - 1, q].astype(F32)
        if step < SHORT:
            rs_out[LONG + step, q] = mine.astype(BF)
            rs[False, step, q] = send(
                rs_out.at[LONG + step, q], rs_in.at[LONG + step, q],
                R_Z + (LONG + step) * NY + q, tab=zz(-1) * NY + y,
            )
        else:
            fz[q] = mine

    def reduce_step(step, term):
        for q in range(NY):
            reduce_long(step, q, term[q * PER : (q + 1) * PER])
            reduce_short(step, q, term[CH + q * PER : CH + (q + 1) * PER])

    def gather_step(step):
        for k in range(NY):
            ring(step, k)

    term = pool(zz(LONG), zz(-SHORT))
    reduce_step(0, term)
    term = pool(zz(LONG - 1), zz(1 - SHORT))
    gather_step(1)
    reduce_step(1, term)

    l_wl.wait()
    n_wide = wl.shape[-1]
    tables = wl.shape[0]
    for w in range(tables):
        wlens = jnp.broadcast_to(wl[w].astype(F32), (128, n_wide)).astype(BF)
        for c in range(n_wide // 128):
            row = lax.broadcasted_iota(jnp.int32, (128, n_wide), 0) + c * 128
            place = lax.broadcasted_iota(jnp.int32, (128, n_wide), 1)
            upto = jnp.where(place <= row, 1.0, 0.0).astype(BF)
            below = jnp.where(place < row, 1.0, 0.0).astype(BF)
            web[w, c] = dot(upto, wlens, NT).astype(jnp.int32)
            wsb[w, c] = dot(below, wlens, NT).astype(jnp.int32)
    l_wr.wait()
    l_wp.wait()
    w_rows = wr.shape[3]
    w_dim = wr.shape[2]
    wlane = lax.broadcasted_iota(jnp.int32, (128, 128), 1)
    parts = []
    for w in range(tables):
        for c in range(n_wide // 128):
            lo = wlane - wsb[w, c]
            hi = wlane - web[w, c]
            for t in range(0, w_rows, 128):
                mask[w, c * 128 : (c + 1) * 128, t : t + 128] = jnp.where(
                    (lo >= -t) & (hi < -t), 1.0, 0.0
                ).astype(BF)
        parts.append(dot(mask[w], wr[w, 0], NT))
    wpooled[...] = jnp.concatenate(parts, axis=1).astype(BF)
    proj = wp[...].reshape(tables * w_dim, wp.shape[2])
    term = (factor * dot(wpooled[...], proj, NN)).astype(BF)
    wterm[...] = term.reshape(wterm.shape)
    ws = send(wterm.at[:, 1 - core], wsib, W_S, col=x * NC + 1 - core)
    for k in range(1, NX):
        xa[k].wait_recv()
    xs = send(cw.at[:, core], cw.at[:, core], X_S, col=x * NC + 1 - core)

    def grads_pair(a, b, i):
        both = jnp.concatenate([ag[a].reshape(CH, -1), ag[b].reshape(CH, -1)], axis=0)
        back[i] = jnp.where(keep, factor * dot(both, npj[0], NT), 0.0).astype(BF)
        grads = dot(jnp.concatenate([pooled[a], pooled[b]], axis=0), both, TN)
        if i == 0:
            ng_acc[...] = grads
        else:
            ng_acc[...] += grads

    def rows_pair(a, b, i):
        sub = lax.broadcasted_iota(jnp.int32, (8, 2 * CH), 0)
        lo = sub - jnp.concatenate([sr[a][:8], sr[b][:8]], axis=1)
        hi = sub - jnp.concatenate([er[a][:8], er[b][:8]], axis=1)
        deep = 512
        for r in range(0, n_rows, deep):
            rows = jnp.concatenate(
                [
                    jnp.where((lo >= -(r + g)) & (hi < -(r + g)), 1.0, 0.0)
                    for g in range(0, deep, 8)
                ],
                axis=0,
            ).astype(BF)
            got = dot(rows, back[i], NN)
            if i > 0:
                got = got + nrg[r : r + deep, :].astype(F32)
            nrg[r : r + deep, :] = got.astype(BF)
            if i == LONG - 1:
                keep_out(nrg.at[r : r + deep], o_nr.at[0, 0, r : r + deep])

    gr = {}

    def wide_step(step):
        one, two = wg[zz(LONG - step)], wg[zz(step - SHORT)]
        if step > 0:
            gr[True, step - 1].wait_recv()
            one = one + wg_in[step - 1].astype(F32)
            gr[False, step - 1].wait_recv()
            two = two + wg_in[LONG + step - 1].astype(F32)
        wg_out[step] = one.astype(BF)
        gr[True, step] = send(wg_out.at[step], wg_in.at[step], G_Z + step, tab=zz(1) * NY + y)
        if step < SHORT:
            wg_out[LONG + step] = two.astype(BF)
            gr[False, step] = send(
                wg_out.at[LONG + step], wg_in.at[LONG + step], G_Z + LONG + step, tab=zz(-1) * NY + y
            )
        else:
            wgz[...] = two

    term = pool(zz(LONG - 2), zz(2 - SHORT))
    gather_step(2)
    reduce_step(2, term)

    ws.wait_recv()
    wx_out[...] = (wterm[:, core].astype(F32) + wsib[...].astype(F32)).astype(BF)
    wx = [None]
    for k in range(1, NX):
        p = lax.rem(x + k, NX)
        wx.append(send(wx_out.at[p], wx_in.at[x], W_X + k, col=p * NC + core))
    wx_in[x] = wx_out[x]

    xs.wait_recv()
    cols = cw[...].reshape(n_wide, -1)
    wg[...] = (factor * dot(wpooled[...], cols, TN)).T.reshape(wg.shape)
    wide_step(0)

    term = pool(zz(LONG - 3), z)
    grads_pair(zz(-1), zz(1), 0)
    rows_pair(zz(-1), zz(1), 0)
    gather_step(3)
    reduce_step(3, term)
    wide_step(1)

    grads_pair(zz(-2), zz(2), 1)
    grads_pair(zz(-3), zz(3), 2)
    rows_pair(zz(-2), zz(2), 1)

    gather_step(LONG)
    grads_pair(zz(-4), z, 3)
    ng_out[...] = (factor * ng_acc[...]).T.astype(BF).reshape(ng_out.shape)
    nx = [None]
    for k in range(1, NX):
        p = lax.rem(x + k, NX)
        nx.append(send(ng_out.at[p], ng_in.at[x], N_X + k, col=p * NC + core))
    ng_in[x] = ng_out[x]
    wide_step(2)

    rows_pair(zz(-3), zz(3), 2)

    for q in range(NY):
        rs[True, LONG - 1, q].wait_recv()
        full = fz[q] + rs_in[LONG - 1, q].astype(F32)
        fz[q] = full
        fy_out[q] = full.astype(BF)

        @pl.when(y != q)
        def _():
            copy(fy_out.at[q], fy_in.at[y], F_Y + q * NY + y, tab=z * NY + q).start()

    fy_in[y] = jnp.zeros(fy_in.shape[1:], BF)
    wide_step(3)

    for k in range(1, NX):
        nx[k].wait_recv()
    nsum = jnp.sum(ng_in[...].astype(F32), axis=0)
    nq_out[...] = nsum.reshape(nq_out.shape)
    me = core * ND + dp
    nq = [
        send(nq_out.at[(1 - core) * ND + dp], nq_in.at[me], N_Q + 1, col=x * NC + 1 - core),
        send(nq_out.at[core * ND + 1 - dp], nq_in.at[me], N_Q + 2, dp=1 - dp),
        send(
            nq_out.at[(1 - core) * ND + 1 - dp], nq_in.at[me], N_Q + 3,
            col=x * NC + 1 - core, dp=1 - dp,
        ),
    ]
    nq_in[me] = nq_out[me]

    wback = (factor * dot(proj, cw[...].reshape(n_wide, -1), NT)).astype(BF)
    for w in range(tables):
        wrg[w, 0] = dot(wback[w * w_dim : (w + 1) * w_dim], mask[w], NN).astype(BF)
        keep_out(wrg.at[w], o_wr.at[w])

    gr[True, LONG - 1].wait_recv()
    wsum = wgz[...] + wg_in[LONG - 1].astype(F32)
    wg2_out[...] = wsum.reshape(wg2_out.shape)
    gy = [None]
    for k in range(1, NYF):
        p = lax.rem(yf + k, NYF)
        gy.append(
            send(wg2_out.at[p], wg2_in.at[yf], G_Y + k, tab=z * NY + p // ND, dp=lax.rem(p, ND))
        )
    wg2_in[yf] = wg2_out[yf]

    rows_pair(zz(-4), z, 3)

    for k in range(1, NY):
        p = lax.rem(y + k, NY)
        copy(fy_out.at[p], fy_in.at[p], F_Y + y * NY + p, tab=z * NY + p).wait_recv()
        copy(fy_out.at[p], fy_in.at[y], F_Y + p * NY + y, tab=z * NY + p).wait_send()
    for k in range(1, NX):
        wx[k].wait_recv()
    total = fz[y] + jnp.sum(fy_in[...].astype(F32), axis=0) + jnp.sum(wx_in[...].astype(F32), axis=0)
    xo[...] = total.astype(BF)
    keep_out(xo, o_x)

    for k in range(1, NYF):
        gy[k].wait_recv()
    wout = jnp.sum(wg2_in[...], axis=0)
    for w in range(tables):
        wgo[w] = wout[:, w * w_dim : (w + 1) * w_dim]
    keep_out(wgo, o_wg)

    for c in nq:
        c.wait_recv()
    ngo[0] = jnp.sum(nq_in[...], axis=0)
    keep_out(ngo, o_ng)

    for c in sent:
        c.wait_send()
    for c in stores:
        c.wait()


def pieces(shape):
    if len(shape) < 4:
        return [()]
    rows = shape[2] // STORE_PARTS
    return [(w, 0, pl.ds(i * rows, rows)) for w in range(shape[0]) for i in range(STORE_PARTS)]


def store(*refs):
    n = len(refs) // 3
    src, dst, held, sem = refs[:n], refs[n : 2 * n], refs[2 * n : 3 * n], refs[3 * n]
    parts = [(i, at) for i in range(n) for at in pieces(src[i].shape)]
    come, go = [], []
    for j, (i, at) in enumerate(parts):
        s, h, d = (r.at[at] if at else r for r in (src[i], held[i], dst[i]))
        come.append(pltpu.make_async_copy(s, h, sem.at[j]))
        go.append(pltpu.make_async_copy(h, d, sem.at[len(parts) + j]))
    for c in come:
        c.start()
    for c, g in zip(come, go):
        c.wait()
        g.start()
    for g in go:
        g.wait()


def body(
    wide_rows,
    wide_lengths,
    narrow_rows,
    narrow_lengths,
    narrow_widths,
    wide_proj,
    narrow_proj,
    cotangent,
):
    out_width = cotangent.shape[1]
    tables, _, w_rows, w_dim = wide_rows.shape
    n_rows, slot = narrow_rows.shape[2:]
    n_wide, n_narrow = wide_lengths.shape[2], narrow_lengths.shape[2]
    factor = (tables + narrow_rows.shape[0] * lax.axis_size("tab")) ** (-0.5)
    rows_t = jnp.transpose(wide_rows, (0, 1, 3, 2))
    wk = tables * w_dim
    v = pltpu.VMEM
    scratch = [
        v((tables, 1, w_dim, w_rows), BF), v(wide_lengths.shape, jnp.int32),
        v(narrow_rows.shape, BF), v(narrow_lengths.shape, jnp.int32),
        v(wide_proj.shape, BF), v(narrow_proj.shape, BF), v(cotangent.shape, BF),
        v((NZ, CH, 128), jnp.int32), v((NZ, CH, 128), jnp.int32),
        v((NZ, 16, 128), jnp.int32), v((NZ, 16, 128), jnp.int32),
        v((tables, n_wide // 128, 128, 128), jnp.int32), v((tables, n_wide // 128, 128, 128), jnp.int32),
        v((NZ, CH, slot), BF), v((tables, n_wide, w_rows), BF), v((n_wide, wk), BF),
        v((NX, NC, PER, out_width), BF), v((NZ, NY, PER, out_width), BF), v((NX, NC, PER, out_width), BF),
        v((LONG + SHORT, NY, PER, out_width), BF), v((LONG + SHORT, NY, PER, out_width), BF),
        v((NX, PER, out_width), BF), v((NX, PER, out_width), BF), v((NX, PER, out_width), BF),
        v((NY, PER, out_width), F32), v((NY, PER, out_width), BF), v((NY, PER, out_width), BF),
        v((NZ, out_width // NZ, wk), F32), v((out_width // NZ, wk), F32),
        v((LONG + SHORT, out_width // NZ, wk), BF), v((LONG + SHORT, out_width // NZ, wk), BF),
        v((NYF, out_width // NZ // NYF, wk), F32), v((NYF, out_width // NZ // NYF, wk), F32),
        v((slot, out_width), F32), v((NX, out_width // NX, slot), BF), v((NX, out_width // NX, slot), BF),
        v((NC * ND, out_width // NX // NC // ND, slot), F32), v((NC * ND, out_width // NX // NC // ND, slot), F32),
        v((LONG, 2 * CH, slot), BF), v((n_rows, slot), BF), v((tables, 1, w_dim, w_rows), BF), v((PER, out_width), BF),
        v((tables, out_width // NZ // NYF, w_dim), F32), v((1, out_width // NX // NC // ND, slot), F32),
        pltpu.SemaphoreType.DMA((N_SEM,)), pltpu.SemaphoreType.DMA((N_SEM,)),
        pltpu.SemaphoreType.DMA((8,)), pltpu.SemaphoreType.DMA((16,)),
    ]
    hbm = pl.BlockSpec(memory_space=pl.ANY)
    smem = pl.BlockSpec(memory_space=pltpu.SMEM)
    s = jax.ShapeDtypeStruct
    outs = pl.pallas_call(
        functools.partial(kernel, factor),
        name="sparse_arch",
        out_shape=(
            s((PER, out_width), BF),
            s((tables, 1, w_dim, w_rows), BF),
            s(narrow_rows.shape, BF),
            s((tables, out_width // NZ // NYF, w_dim), F32),
            s((1, out_width // NX // NC // ND, slot), F32),
        ),
        in_specs=[hbm, hbm, hbm, hbm, smem, hbm, hbm, hbm],
        out_specs=(hbm,) * 5,
        scratch_shapes=scratch,
        compiler_params=pltpu.CompilerParams(
            collective_id=0, has_side_effects=True, vmem_limit_bytes=VMEM
        ),
    )(rows_t, wide_lengths, narrow_rows, narrow_lengths, narrow_widths, wide_proj, narrow_proj, cotangent)
    cross, wide_t, narrow, wide_g, narrow_g = pl.pallas_call(
        store,
        name="store",
        out_shape=[s(o.shape, o.dtype) for o in outs],
        in_specs=[hbm] * len(outs),
        out_specs=[hbm] * len(outs),
        scratch_shapes=[v(o.shape, o.dtype) for o in outs] + [pltpu.SemaphoreType.DMA((2 * sum(len(pieces(o.shape)) for o in outs),))],
        compiler_params=pltpu.CompilerParams(vmem_limit_bytes=VMEM),
    )(*outs)
    return (
        cross,
        jnp.transpose(wide_t, (0, 1, 3, 2)),
        narrow,
        jnp.transpose(wide_g, (0, 2, 1)),
        jnp.transpose(narrow_g, (0, 2, 1)),
    )


def solution(mesh):
    in_specs = (
        P(None, ("tab", "dp"), None, "col"),
        P(None, ("tab", "dp"), None),
        P("tab", ("col", "dp"), None, None),
        P("tab", ("col", "dp"), None),
        P("tab"),
        P(None, "col", None),
        P("tab", None, None),
        P(("col", "tab", "dp"), None),
    )
    out_specs = (
        P(("col", "tab", "dp"), None),
        P(None, ("tab", "dp"), None, "col"),
        P("tab", ("col", "dp"), None, None),
        P(None, "col", ("tab", "dp")),
        P("tab", None, ("col", "dp")),
    )
    return jax.shard_map(body, mesh=mesh, in_specs=in_specs, out_specs=out_specs, check_vma=False)
```
